256 devices in a mesh: dp: 2 (over x_hi), ctx: 32 (over y, z), mp: 4 (over x_lo, core).
Axes of the slice: x: 4 (x_hi: 2, x_lo: 2; x = x_hi * 2 + x_lo), y: 4, z: 8, core: 2. Of those that a mesh axis runs over, the one named last changes fastest.
Arguments:
- queries: bfloat16 [16384, 2560], P(('dp', 'ctx'), 'mp'), parts along dimension 0, may hold values from -6 to 6
- keys: bfloat16 [16384, 512], P(('dp', 'ctx'), 'mp'), parts along dimension 0, may hold values from -6 to 6
- values: bfloat16 [16384, 512], P(('dp', 'ctx'), 'mp'), parts along dimension 0, may hold values from -6 to 6
- out_weight: bfloat16 [2560, 5120], P('mp'), may hold values from -0.125 to 0.125
- block_order: int32 [128], P('dp'), parts along dimension 0, may hold values from 0 to 63, each once
- doc_lengths: int32 [16], P('dp'), parts along dimension 0, may hold values from 1 to 2048, 8192 in all
- reveal_step: int32 [128, 64], P('dp'), parts along dimension 0, may hold values from 0 to 16, as said below
- train_step: int32 [2], P('dp'), parts along dimension 0, may hold values from 1 to 15
Outputs:
- mixed: bfloat16 [16384, 5120], P(('dp', 'ctx'), 'mp'), parts along dimension 0
The draws below stay inside these ranges and needn't reach their ends.
There are 2 independent parts, one for each index of `dp`. The reference program is written for one: setup_inputs(seed, part) draws one part's arguments, and reference() takes and returns one part's arrays. A program takes and returns all parts, laid end to end along the dimension named above; an argument that names none is the same for every part. Nothing has to cross between parts.
Inputs may be any that keep to these rules, and one draw needn't show every extreme that they name: `reveal_step`: 0 where the key block does not come after the query block, between 1 and 16 where it does.
All inputs are finite; a program needn't handle non-finite values.
Results may differ from the reference program's by a relative error of at most 0.017.
Values may be sent and summed in bfloat16 or wider, within the bound.
No kernel may reach another device: no remote copies, remote signals or barrier semaphores. Data moves between devices by JAX's collectives and lax.ppermute only.
A program may use at most 64 MiB of HBM per device.

```python
import math
import jax
import jax.numpy as jnp
import numpy as np
from jax import lax

D = 5120
HEAD_WIDTH = 128
QUERY_HEAD_COUNT = 20
KEY_VALUE_HEADS = 4
BLK = 128
ANNEAL = 16
DOCS = 8
PACKED_TOKENS = 8192
NB = 64
SHARED_QUERIES = 5
MOST = 2048


def draw_queries(key, part):
    key = jax.random.fold_in(key, 11)
    attention_output = jnp.clip(jax.random.normal(key, (PACKED_TOKENS, QUERY_HEAD_COUNT * HEAD_WIDTH)), -4.0, 4.0)
    return attention_output.astype(jnp.bfloat16)


def draw_keys(key, part):
    key = jax.random.fold_in(key, 13)
    attention_output = jnp.clip(jax.random.normal(key, (PACKED_TOKENS, KEY_VALUE_HEADS * HEAD_WIDTH)), -4.0, 4.0)
    return attention_output.astype(jnp.bfloat16)


def draw_reveal_step(key, part):
    key = jax.random.fold_in(key, 7)
    steps_drawn = jax.random.randint(key, (NB, NB), 1, ANNEAL + 1)
    query_ids = jnp.arange(NB)[:, None]
    key_ids = jnp.arange(NB)[None, :]
    steps_drawn = jnp.where(key_ids <= query_ids, 0, steps_drawn)
    steps_drawn = jnp.where((query_ids == 0) & (key_ids == NB - 1), ANNEAL, steps_drawn)
    return steps_drawn.astype(jnp.int32)


def level_of(own_key, dims, pieces, low, largest):
    def one(position, blocks):
        steps = jax.random.uniform(jax.random.fold_in(jax.random.fold_in(own_key, 6), position), (blocks,), jnp.float32, low / len(pieces), largest / len(pieces))
        return jnp.repeat(jnp.exp(steps), dims[position] // blocks).reshape((-1,) + (1,) * (len(dims) - position - 1))

    factor_of = one(*pieces[0])
    for cut in pieces[1:]:
        factor_of = factor_of * one(*cut)
    return factor_of


def length_profile(amount, total, bound, skew):
    weights = [(1 << 20) // math.isqrt(standing ** skew) + 1 for standing in range(2, amount + 1)]
    spare, holding = total - bound - (amount - 1), [1] * (amount - 1)
    while spare > 0:
        candidates = [i for i in range(amount - 1) if holding[i] < bound]
        mass, remaining = sum([weights[i] for i in candidates]), spare
        for i in candidates:
            more = min(bound - holding[i], max(1, remaining * weights[i] // mass), spare)
            holding[i] = holding[i] + more
            spare = spare - more
    return np.array([bound] + holding)


def ragged_sizes(stream_key, count, total, bound, skew):
    if count == 2:
        one = jax.random.randint(stream_key, (), max(1, total - bound), min(bound, total - 1) + 1)
        return jnp.stack([one, total - one])
    lengths = jnp.asarray(length_profile(count, total, bound, skew), jnp.int32)
    couples = (count - 1) // 2
    giver, taker = lengths[1:1 + 2 * couples:2], lengths[2:2 + 2 * couples:2]
    room = jnp.minimum(giver - 1, bound - taker)
    moved = jax.random.randint(jax.random.fold_in(stream_key, 1), (couples,), 0, 1 << 20) % (room + 1)
    lengths = lengths.at[1:1 + 2 * couples:2].set(giver - moved).at[2:2 + 2 * couples:2].set(taker + moved)
    return lengths[jax.random.permutation(jax.random.fold_in(stream_key, 2), count)]


def scatter_about(rng, dims, width, reach, cuts=(), kind=jnp.bfloat16):
    entries = width * jax.random.normal(rng, dims, jnp.float32)
    if cuts:
        entries = entries * level_of(rng, dims, cuts, -0.22, 0.18)
    return jnp.clip(entries, -reach, reach).astype(kind)


def setup_inputs(seed: int = 0, part: int = 0) -> dict:
    arg_keys = jax.random.split(jax.random.key(seed), 9)
    own_keys = jax.random.split(jax.random.fold_in(arg_keys[8], part), 9)
    queries = draw_queries(jax.random.fold_in(jax.random.fold_in(arg_keys[8], part), 71), part)
    keys = draw_keys(jax.random.fold_in(jax.random.fold_in(arg_keys[8], part), 71), part)
    values = scatter_about(own_keys[2], (PACKED_TOKENS, KEY_VALUE_HEADS * HEAD_WIDTH), 1.0, 6.0, ((0, 32), (1, 4)))
    out_weight = scatter_about(arg_keys[3], (QUERY_HEAD_COUNT * HEAD_WIDTH, D), (QUERY_HEAD_COUNT * HEAD_WIDTH) ** -0.5, 0.125, ((0, 4),))
    block_order = jax.random.permutation(own_keys[4], NB).astype(jnp.int32)
    doc_lengths = ragged_sizes(own_keys[5], DOCS, PACKED_TOKENS, MOST, 1).astype(jnp.int32)
    reveal_step = draw_reveal_step(jax.random.fold_in(jax.random.fold_in(arg_keys[8], part), 71), part)
    train_step = jax.random.randint(own_keys[7], (1,), 1, ANNEAL).astype(jnp.int32)
    return {"queries": queries, "keys": keys, "values": values, "out_weight": out_weight, "block_order": block_order, "doc_lengths": doc_lengths, "reveal_step": reveal_step, "train_step": train_step}


def positions(block_order, row_count):
    row_ids = jnp.arange(row_count, dtype=jnp.int32)
    return block_order[row_ids // BLK] * BLK + row_ids % BLK

def documents(slot_pos, doc_lengths):
    doc_ends = jnp.cumsum(doc_lengths)
    return lax.optimization_barrier(jnp.sum((slot_pos[:, None] >= doc_ends[None, :]).astype(jnp.int32), axis=1))

def reference(queries, keys, values, out_weight, block_order, doc_lengths, reveal_step, train_step):
    slot_pos = positions(block_order, PACKED_TOKENS)
    slot_doc = documents(slot_pos, doc_lengths)
    slot_block = slot_pos // BLK
    scaling = 1.0 / math.sqrt(HEAD_WIDTH)
    complete_queries = queries.astype(jnp.float32).reshape(PACKED_TOKENS, KEY_VALUE_HEADS, SHARED_QUERIES, HEAD_WIDTH)
    complete_keys = keys.astype(jnp.float32).reshape(PACKED_TOKENS, KEY_VALUE_HEADS, HEAD_WIDTH)
    complete_values = values.astype(jnp.float32).reshape(PACKED_TOKENS, KEY_VALUE_HEADS, HEAD_WIDTH)
    row_block = min(PACKED_TOKENS, 256)

    def one_block(first_row):
        query_part = lax.dynamic_slice_in_dim(complete_queries, first_row, row_block, 0)
        query_doc = lax.dynamic_slice_in_dim(slot_doc, first_row, row_block, 0)
        query_block = lax.dynamic_slice_in_dim(slot_block, first_row, row_block, 0)
        allowed = (query_doc[:, None] == slot_doc[None, :]) & (reveal_step[query_block][:, slot_block] <= train_step[0])
        scores = jnp.einsum('qhgd,khd->hgqk', query_part, complete_keys) * scaling
        row_max = lax.optimization_barrier(jnp.max(jnp.where(allowed, scores, -jnp.inf), axis=3))
        probs = jnp.where(allowed, jnp.exp(scores - row_max[..., None]), 0.0)
        totals = lax.optimization_barrier(jnp.sum(probs, axis=3))
        rounded = lax.optimization_barrier(probs.astype(jnp.bfloat16))
        mixed_heads = jnp.einsum('hgqk,khd->qhgd', rounded.astype(jnp.float32), complete_values)
        mixed_heads = mixed_heads / jnp.transpose(totals, (2, 0, 1))[..., None]
        return mixed_heads.reshape(row_block, QUERY_HEAD_COUNT * HEAD_WIDTH).astype(jnp.bfloat16)
    starts = (jnp.arange(PACKED_TOKENS // row_block) * row_block).astype(jnp.int32)
    attended = lax.map(one_block, starts).reshape(PACKED_TOKENS, QUERY_HEAD_COUNT * HEAD_WIDTH)
    return jnp.dot(attended, out_weight, preferred_element_type=jnp.float32).astype(jnp.bfloat16)
```

```python
import math

import jax
import jax.numpy as jnp
from jax import lax
from jax.experimental import pallas as pl
from jax.experimental.pallas import tpu as pltpu
from jax.sharding import Mesh
from jax.sharding import PartitionSpec as P

HEAD_WIDTH = 128
BLK = 128
NY, NZ, NX, NC = 4, 8, 2, 2
RANKS = NY * NZ
SLOTS = 2 * RANKS
MASKED = -1e30
LOWEST = -1e20


def moved(x, dy, dz):
    route = [(((i // NZ + dy) % NY) * NZ + (i % NZ + dz) % NZ, i) for i in range(RANKS)]
    return lax.ppermute(x, ("y", "z"), route)


def gathered(kv):
    rows = kv.shape[0] // 2
    centre = {0: kv}
    for j in (2, -2, 1, -1, 4, 3, -3):
        centre[j % 8] = moved(kv, 2 * j, j)
    key_of, value_of = {}, {}
    for j, block in centre.items():
        at = ((2 * j) % NY, j % NZ)
        key_of[at], value_of[at] = block[:rows], block[rows:]
    for group in ((0, 2, 6, 1, 7), (4, 3, 5)):
        blocks = [centre[j] for j in group]
        both = jnp.concatenate(blocks)
        only_keys = jnp.concatenate([b[:rows] for b in blocks])
        only_values = jnp.concatenate([b[rows:] for b in blocks])
        for dy in (1, -1):
            got = moved(both, dy, 0)
            for i, j in enumerate(group):
                at = ((2 * j + dy) % NY, j % NZ)
                key_of[at] = got[2 * i * rows : (2 * i + 1) * rows]
                value_of[at] = got[(2 * i + 1) * rows : (2 * i + 2) * rows]
        got = moved(only_keys, 0, 1)
        for i, j in enumerate(group):
            key_of[((2 * j) % NY, (j + 1) % NZ)] = got[i * rows : (i + 1) * rows]
        got = moved(only_values, 0, -1)
        for i, j in enumerate(group):
            value_of[((2 * j) % NY, (j - 1) % NZ)] = got[i * rows : (i + 1) * rows]
    order = [(dy, dz) for dy in range(NY) for dz in range(NZ)]
    return jnp.concatenate([key_of[at] for at in order]), jnp.concatenate([value_of[at] for at in order])


def plan_kernel(place, order, lengths, reveal, step, lists, counts):
    y, z = place[0], place[1]
    for t in range(2):
        block = order[2 * (y * NZ + z) + t]
        first, last = block * BLK, block * BLK + BLK - 1
        end = jnp.int32(0)
        low, high, first_end = jnp.int32(0), jnp.int32(0), jnp.int32(0)
        for d in range(lengths.shape[0]):
            begin = end
            end = end + lengths[d]
            holds_first = (begin <= first) & (first < end)
            low = jnp.where(holds_first, begin, low)
            first_end = jnp.where(holds_first, end, first_end)
            high = jnp.where((begin <= last) & (last < end), end, high)
        one_doc = first_end == high

        def seen(s, key_block):
            begin = key_block * BLK
            near = (begin < high) & (begin + BLK > low)
            whole = one_doc & (begin >= low) & (begin + BLK <= high)
            return near & (reveal[block, key_block] <= step[0]), whole

        def key_block_of(s):
            dy, dz = s // (2 * NZ), (s // 2) % NZ
            rank = ((y + dy) % NY) * NZ + (z + dz) % NZ
            return order[2 * rank + s % 2]

        def put(at, s, key_block):
            lists[t, 0, at] = s
            lists[t, 1, at] = key_block

        def whole_ones(s, n):
            key_block = key_block_of(s)
            near, whole = seen(s, key_block)
            take = near & whole

            @pl.when(take)
            def _():
                put(n, s, key_block)

            return n + take.astype(jnp.int32)

        def masked_ones(s, n):
            key_block = key_block_of(s)
            near, whole = seen(s, key_block)
            take = near & jnp.logical_not(whole)

            @pl.when(take)
            def _():
                put(n, s, key_block)

            return n + take.astype(jnp.int32)

        n_whole = lax.fori_loop(0, SLOTS, whole_ones, jnp.int32(0))
        n = lax.fori_loop(0, SLOTS, masked_ones, n_whole)

        @pl.when(n % 2 == 1)
        def _():
            put(n, 0, SLOTS)

        counts[t, 0] = n_whole // 2
        counts[t, 1] = (n + 1) // 2


def attention_kernel(lists, counts, place, order, lengths, q_ref, k_ref, v_ref, out_ref, scores, top, total, acc):
    heads = q_ref.shape[1] // HEAD_WIDTH
    scale = math.log2(math.e) / math.sqrt(HEAD_WIDTH)

    def doc_of(pos):
        doc = jnp.zeros(pos.shape, jnp.int32)
        end = jnp.int32(0)
        for d in range(lengths.shape[0]):
            end = end + lengths[d]
            doc = doc + (pos >= end).astype(jnp.int32)
        return doc

    for t in range(2):
        block = order[2 * (place[0] * NZ + place[1]) + t]
        rows = pl.ds(t * BLK, BLK)
        q = jnp.concatenate([q_ref[rows, h * HEAD_WIDTH : (h + 1) * HEAD_WIDTH] for h in range(heads)])
        q_doc = doc_of(block * BLK + lax.broadcasted_iota(jnp.int32, (BLK, BLK), 0))
        top[...] = jnp.full(top.shape, LOWEST, jnp.float32)
        n_whole, n = counts[t, 0], counts[t, 1]

        def two(ref, i):
            return jnp.concatenate(
                [ref[pl.ds(pl.multiple_of(lists[t, 0, 2 * i + e] * BLK, BLK), BLK), :] for e in range(2)]
            )

        def dots(i):
            return lax.dot_general(q, two(k_ref, i), (((1,), (1,)), ((), ())), preferred_element_type=jnp.float32)

        def whole_pair(i, carry):
            s = dots(i)
            scores[i] = s
            top[...] = jnp.maximum(top[...], jnp.maximum(s[:, :BLK], s[:, BLK:]))
            return carry

        def masked_pair(i, carry):
            s = dots(i)
            lane = lax.broadcasted_iota(jnp.int32, (1, BLK), 1)
            for e in range(2):
                k_doc = doc_of(lists[t, 1, 2 * i + e] * BLK + lane)
                allowed = q_doc == k_doc
                for h in range(heads):
                    part = jnp.where(
                        allowed, s[h * BLK : (h + 1) * BLK, e * BLK : (e + 1) * BLK], MASKED
                    )
                    scores[i, pl.ds(h * BLK, BLK), pl.ds(e * BLK, BLK)] = part
                    top[pl.ds(h * BLK, BLK), :] = jnp.maximum(top[pl.ds(h * BLK, BLK), :], part)
            return carry

        lax.fori_loop(0, n_whole, whole_pair, 0)
        lax.fori_loop(n_whole, n, masked_pair, 0)
        top[...] = jnp.broadcast_to(jnp.max(top[...], axis=1, keepdims=True) * scale, top.shape)
        total[...] = jnp.zeros(total.shape, jnp.float32)
        acc[...] = jnp.zeros(acc.shape, jnp.float32)

        def weigh(i, carry):
            s = scores[i]
            m = top[...]
            p0 = jnp.exp2(s[:, :BLK] * scale - m)
            p1 = jnp.exp2(s[:, BLK:] * scale - m)
            total[...] += p0 + p1
            p = jnp.concatenate([p0.astype(jnp.bfloat16), p1.astype(jnp.bfloat16)], axis=1)
            acc[...] += jnp.dot(p, two(v_ref, i), preferred_element_type=jnp.float32)
            return carry

        lax.fori_loop(0, n, weigh, 0)
        attended = (acc[...] / jnp.sum(total[...], axis=1, keepdims=True)).astype(jnp.bfloat16)
        for h in range(heads):
            out_ref[rows, h * HEAD_WIDTH : (h + 1) * HEAD_WIDTH] = attended[h * BLK : (h + 1) * BLK]


def attention(queries, keys, values, block_order, doc_lengths, reveal_step, train_step):
    place = jnp.stack([lax.axis_index("y"), lax.axis_index("z")]).astype(jnp.int32)
    smem = pl.BlockSpec(memory_space=pltpu.SMEM)
    vmem = pl.BlockSpec(memory_space=pltpu.VMEM)
    lists, counts = pl.pallas_call(
        plan_kernel,
        out_shape=(
            jax.ShapeDtypeStruct((2, 2, SLOTS + 2), jnp.int32),
            jax.ShapeDtypeStruct((2, 2), jnp.int32),
        ),
        in_specs=[smem] * 5,
        out_specs=(smem, smem),
        name="plan",
    )(place, block_order, doc_lengths, reveal_step, train_step)
    rows = queries.shape[1] // HEAD_WIDTH * BLK
    return pl.pallas_call(
        attention_kernel,
        out_shape=jax.ShapeDtypeStruct(queries.shape, jnp.bfloat16),
        in_specs=[smem] * 5 + [vmem] * 3,
        out_specs=vmem,
        scratch_shapes=[
            pltpu.VMEM((17, rows, 2 * BLK), jnp.float32),
            pltpu.VMEM((rows, BLK), jnp.float32),
            pltpu.VMEM((rows, BLK), jnp.float32),
            pltpu.VMEM((rows, BLK), jnp.float32),
        ],
        compiler_params=pltpu.CompilerParams(vmem_limit_bytes=40 * 2**20),
        cost_estimate=pl.CostEstimate(flops=10**9, bytes_accessed=10**7, transcendentals=3 * 10**6),
        name="attention",
    )(lists, counts, place, block_order, doc_lengths, queries, keys, values)


def swapped(x, axis):
    return lax.ppermute(x, axis, [(0, 1), (1, 0)])


def per_device(queries, keys, values, out_weight, block_order, doc_lengths, reveal_step, train_step):
    x, core = lax.axis_index("x"), lax.axis_index("core")
    width = out_weight.shape[1] // (NX * NC)
    columns = out_weight.reshape(out_weight.shape[0], NX, NC, width)
    own_weight = lax.dynamic_index_in_dim(columns, core, 2, keepdims=False)
    other_weight = swapped(lax.dynamic_index_in_dim(columns, 1 - core, 2, keepdims=False), "core")
    all_keys, all_values = gathered(jnp.concatenate([keys, values]))
    attended = attention(queries, all_keys, all_values, block_order, doc_lengths, reveal_step, train_step)
    other_attended = swapped(attended, "core")

    def share(chip):
        return jnp.dot(
            attended, lax.dynamic_index_in_dim(own_weight, chip, 1, keepdims=False), preferred_element_type=jnp.float32
        ) + jnp.dot(
            other_attended,
            lax.dynamic_index_in_dim(other_weight, chip, 1, keepdims=False),
            preferred_element_type=jnp.float32,
        )

    sent = swapped(share(1 - x).astype(jnp.bfloat16), "x")
    return (share(x) + sent.astype(jnp.float32)).astype(jnp.bfloat16)


def solution(mesh):
    fine = Mesh(mesh.devices.reshape(mesh.devices.shape[0], NY, NZ, NX, NC), ("dp", "y", "z", "x", "core"))
    rows, heads = ("dp", "y", "z"), ("x", "core")
    in_specs = (
        P(rows, heads),
        P(rows, heads),
        P(rows, heads),
        P(heads, None),
        P("dp"),
        P("dp"),
        P("dp", None),
        P("dp"),
    )
    return jax.shard_map(per_device, mesh=fine, in_specs=in_specs, out_specs=P(rows, heads), check_vma=False)
```

```python
import functools
import math

import jax
import jax.numpy as jnp
import numpy as np
from jax import lax
from jax.experimental import pallas as pl
from jax.experimental.pallas import tpu as pltpu
from jax.sharding import Mesh
from jax.sharding import PartitionSpec as P

HEAD_WIDTH = 128
BLK = 128
NY, NZ, NX, NC = 4, 8, 2, 2
RANKS = NY * NZ
SLOTS = 2 * RANKS
CENTRES = ((0, 0), (0, 4), (2, 2), (2, -2))
STEPS = ((1, 0), (-1, 0), (0, 1), (0, -1))
PICKS = (((3, 0), (4, 0), (1, 0)), ((4, 1), (3, 0), (2, 1)), ((1, 1), (2, 1), (3, 0)), ((2, 0), (1, 1), (4, 0)))


def offsets():
    near = [[(cy + sy, cz + sz) for cy, cz in CENTRES] for sy, sz in ((0, 0), *STEPS)]
    last = [(near[n][m][0] + sy, near[n][m][1] + sz) for (sy, sz), picks in zip(STEPS, PICKS) for n, m in picks]
    every = [(dy % NY, dz % NZ) for dy, dz in [o for group in near for o in group] + last]
    assert sorted(every) == [(dy, dz) for dy in range(NY) for dz in range(NZ)]
    return every


NEAR = 20


MASKED = -1e30
LOWEST = -1e20


def moved(x, dy, dz):
    route = [(((i // NZ + dy) % NY) * NZ + (i % NZ + dz) % NZ, i) for i in range(RANKS)]
    return lax.ppermute(x, ("y", "z"), route)


def first_round(kv):
    return jnp.concatenate([kv] + [moved(kv, *c) for c in CENTRES[1:]])


def second_round(centres):
    return [centres] + [moved(centres, *s) for s in STEPS]


def third_round(near, rows):
    return [
        moved(jnp.concatenate([near[n][m * rows : (m + 1) * rows] for n, m in picks]), *step)
        for step, picks in zip(STEPS, PICKS)
    ]


COUNTS, OWN, ENDS, LISTS = 0, 8, 16, 64
LONGEST = SLOTS + 2


def listed(l, through_mask, which, at):
    return LISTS + ((2 * l + through_mask) * 2 + which) * LONGEST + at


def plan_kernel(place, ranks, order, lengths, reveal, step, plan):
    y, z = place[0], place[1]
    now = step[0]
    own, low, high, one_doc = [], [], [], []
    for t in range(2):
        block = order[2 * (y * NZ + z) + t]
        first, last = block * BLK, block * BLK + BLK - 1
        begin = jnp.int32(0)
        low_t, first_end, last_end = jnp.int32(0), jnp.int32(0), jnp.int32(0)
        for d in range(lengths.shape[0]):
            end = begin + lengths[d]
            plan[ENDS + d] = end
            holds = (begin <= first) & (first < end)
            low_t = jnp.where(holds, begin, low_t)
            first_end = jnp.where(holds, end, first_end)
            last_end = jnp.where((begin <= last) & (last < end), end, last_end)
            begin = end
        plan[OWN + t] = block
        own.append(block)
        low.append(low_t)
        high.append(last_end)
        one_doc.append(first_end == last_end)

    def slot(first_rank, j, n):
        i = lax.shift_right_logical(j, 1)
        e = jnp.bitwise_and(j, 1)
        key_block = order[2 * ranks[first_rank + i] + e]
        row = i * (4 * BLK) + e * BLK
        begin = key_block * BLK
        n = list(n)
        for t in range(2):
            near = (begin < high[t]) & (begin + BLK > low[t]) & (reveal[own[t], key_block] <= now)
            inside = one_doc[t] & (begin >= low[t]) & (begin + BLK <= high[t])
            l = t if first_rank == 0 else 2 + t
            for m, take in enumerate((near & inside, near & jnp.logical_not(inside))):
                at = n[2 * t + m]
                plan[listed(l, m, 0, at)] = row
                plan[listed(l, m, 1, at)] = key_block
                n[2 * t + m] = at + take.astype(jnp.int32)
        return tuple(n)

    for stage, (first_rank, n_ranks) in enumerate(((0, NEAR), (NEAR, RANKS - NEAR))):
        n = lax.fori_loop(0, 2 * n_ranks, functools.partial(slot, first_rank), (jnp.int32(0),) * 4, unroll=2)
        for t in range(2):
            l = 2 * stage + t
            n_whole, n_masked = n[2 * t], n[2 * t + 1]
            odd = jnp.bitwise_and(n_whole, 1)
            kept = n_whole - odd
            for which in range(2):
                plan[listed(l, 1, which, n_masked)] = plan[listed(l, 0, which, kept)]
            n_masked = n_masked + odd
            plan[listed(l, 1, 0, n_masked)] = 0
            plan[listed(l, 1, 1, n_masked)] = SLOTS
            plan[COUNTS + 2 * l] = lax.shift_right_logical(n_whole, 1)
            plan[COUNTS + 2 * l + 1] = lax.shift_right_logical(n_masked + 1, 1)


def attention_kernel(plan, q_ref, kv, *refs, stage, docs):
    heads = q_ref.shape[1] // HEAD_WIDTH
    scale = math.log2(math.e) / math.sqrt(HEAD_WIDTH)
    if stage == 0:
        top_out, total_out, acc_out, scores, top = refs
    else:
        top_in, total_in, acc_in, out_ref, scores, top, total_out, acc_out = refs

    def doc_of(pos):
        return sum((pos >= plan[ENDS + d]).astype(jnp.int32) for d in range(docs))

    for t in range(2):
        l = 2 * stage + t
        block = plan[OWN + t]
        rows = pl.ds(t * BLK, BLK)
        q = jnp.concatenate([q_ref[rows, h * HEAD_WIDTH : (h + 1) * HEAD_WIDTH] for h in range(heads)])
        q_doc = doc_of(block * BLK + lax.broadcasted_iota(jnp.int32, (BLK, BLK), 0))
        top[...] = jnp.full(top.shape, LOWEST, jnp.float32) if stage == 0 else top_in[t]
        total, acc = (total_out.at[t], acc_out.at[t]) if stage == 0 else (total_out, acc_out)
        n_whole, n_masked = plan[COUNTS + 2 * l], plan[COUNTS + 2 * l + 1]

        def two(through_mask, i, start):
            return jnp.concatenate(
                [
                    kv[pl.ds(pl.multiple_of(plan[listed(l, through_mask, 0, 2 * i + e)] + start, BLK), BLK), :]
                    for e in range(2)
                ]
            )

        def dots(through_mask, i):
            return lax.dot_general(
                q, two(through_mask, i, 0), (((1,), (1,)), ((), ())), preferred_element_type=jnp.float32
            )

        def whole_pair(i, carry):
            s = dots(0, i)
            scores[i] = s
            top[...] = jnp.maximum(top[...], jnp.maximum(s[:, :BLK], s[:, BLK:]))
            return carry

        def masked_pair(i, carry):
            s = dots(1, i)
            lane = lax.broadcasted_iota(jnp.int32, (1, BLK), 1)
            for e in range(2):
                k_doc = doc_of(plan[listed(l, 1, 1, 2 * i + e)] * BLK + lane)
                allowed = q_doc == k_doc
                for h in range(heads):
                    part = jnp.where(
                        allowed, s[h * BLK : (h + 1) * BLK, e * BLK : (e + 1) * BLK], MASKED
                    )
                    scores[n_whole + i, pl.ds(h * BLK, BLK), pl.ds(e * BLK, BLK)] = part
                    top[pl.ds(h * BLK, BLK), :] = jnp.maximum(top[pl.ds(h * BLK, BLK), :], part)
            return carry

        lax.fori_loop(0, n_whole, whole_pair, 0)
        lax.fori_loop(0, n_masked, masked_pair, 0)
        best = jnp.broadcast_to(jnp.max(top[...], axis=1, keepdims=True), top.shape)
        if stage == 0:
            top_out[t] = best
            total[...] = jnp.zeros(total.shape, jnp.float32)
            acc[...] = jnp.zeros(acc.shape, jnp.float32)
        else:
            factor = jnp.exp2((top_in[t] - best) * scale)
            total[...] = total_in[t] * factor
            acc[...] = acc_in[t] * factor
        top[...] = best * scale

        def weigh(through_mask, at, i, carry):
            s = scores[at + i]
            m = top[...]
            p0 = jnp.exp2(s[:, :BLK] * scale - m)
            p1 = jnp.exp2(s[:, BLK:] * scale - m)
            total[...] += p0 + p1
            p = jnp.concatenate([p0.astype(jnp.bfloat16), p1.astype(jnp.bfloat16)], axis=1)
            acc[...] += jnp.dot(p, two(through_mask, i, 2 * BLK), preferred_element_type=jnp.float32)
            return carry

        lax.fori_loop(0, n_whole, functools.partial(weigh, 0, 0), 0)
        lax.fori_loop(0, n_masked, functools.partial(weigh, 1, n_whole), 0)
        if stage == 1:
            attended = (acc[...] / jnp.sum(total[...], axis=1, keepdims=True)).astype(jnp.bfloat16)
            for h in range(heads):
                out_ref[rows, h * HEAD_WIDTH : (h + 1) * HEAD_WIDTH] = attended[h * BLK : (h + 1) * BLK]


SMEM = pl.BlockSpec(memory_space=pltpu.SMEM)
VMEM = pl.BlockSpec(memory_space=pltpu.VMEM)


def planned(place, ranks, block_order, doc_lengths, reveal_step, train_step):
    return pl.pallas_call(
        plan_kernel,
        out_shape=jax.ShapeDtypeStruct((listed(4, 0, 0, 0),), jnp.int32),
        in_specs=[SMEM] * 6,
        out_specs=SMEM,
        name="plan",
    )(place, ranks, block_order, doc_lengths, reveal_step, train_step)


def attention(stage, plan, docs, queries, kv, before=()):
    rows = queries.shape[1] // HEAD_WIDTH * BLK
    running = jax.ShapeDtypeStruct((2, rows, HEAD_WIDTH), jnp.float32)
    held = pltpu.VMEM((rows, HEAD_WIDTH), jnp.float32)
    return pl.pallas_call(
        functools.partial(attention_kernel, stage=stage, docs=docs),
        out_shape=(running,) * 3 if stage == 0 else jax.ShapeDtypeStruct(queries.shape, jnp.bfloat16),
        in_specs=[SMEM] + [VMEM] * (2 + len(before)),
        out_specs=(VMEM,) * 3 if stage == 0 else VMEM,
        scratch_shapes=[pltpu.VMEM((17, rows, 2 * BLK), jnp.float32)] + [held] * (1 if stage == 0 else 3),
        compiler_params=pltpu.CompilerParams(vmem_limit_bytes=15 * 2**20),
        cost_estimate=pl.CostEstimate(flops=10**9, bytes_accessed=10**7, transcendentals=3 * 10**6),
        name="attention_%d" % stage,
    )(plan, queries, kv, *before)


def swapped(x, axis):
    return lax.ppermute(x, axis, [(0, 1), (1, 0)])


def from_both_sides(x):
    ring = 2 * NX
    route = [(((i + (1, -1)[c]) % ring) * NC + c, i * NC + c) for i in range(ring) for c in range(NC)]
    return lax.ppermute(x, ("dp", "x", "core"), route)


def project_kernel(at, heads, weight, *refs):
    *before, out_ref = refs
    width = out_ref.shape[1]
    columns = pl.ds(pl.multiple_of(at[0] * width, width), width)
    total = jnp.dot(heads[...], weight[:, columns], preferred_element_type=jnp.float32)
    if before:
        total = before[0][...] + total
    out_ref[...] = total.astype(out_ref.dtype)


def projected(heads, weight, column, width, dtype, before=()):
    rows, depth = heads.shape
    return pl.pallas_call(
        project_kernel,
        out_shape=jax.ShapeDtypeStruct((rows, width), dtype),
        in_specs=[SMEM] + [VMEM] * (2 + len(before)),
        out_specs=VMEM,
        compiler_params=pltpu.CompilerParams(vmem_limit_bytes=12 * 2**20),
        cost_estimate=pl.CostEstimate(
            flops=2 * rows * width * depth, bytes_accessed=2 * width * depth, transcendentals=0
        ),
        name="project",
    )(column.reshape(1).astype(jnp.int32), heads, weight, *before)


def per_device(queries, keys, values, out_weight, block_order, doc_lengths, reveal_step, train_step):
    x, core = lax.axis_index("x"), lax.axis_index("core")
    y, z = lax.axis_index("y"), lax.axis_index("z")
    width = out_weight.shape[1] // (NX * NC)
    place = jnp.stack([y, z]).astype(jnp.int32)
    by_offset = np.array(offsets(), np.int32)
    ranks = ((by_offset[:, 0] + y) % NY * NZ + (by_offset[:, 1] + z) % NZ).astype(jnp.int32)

    kv = jnp.concatenate([keys, values])
    centres = first_round(kv)
    plan = planned(place, ranks, block_order, doc_lengths, reveal_step, train_step)
    weight_1 = swapped(out_weight, "core")
    centres, weight_1, plan = lax.optimization_barrier((centres, weight_1, plan))
    out_weight, plan = lax.optimization_barrier((out_weight, plan))
    beside = from_both_sides(lax.dynamic_slice_in_dim(out_weight, (1 - x) * NC * width, NC * width, 1))
    near = second_round(centres)
    last = third_round(near, kv.shape[0])
    running = attention(0, plan, doc_lengths.shape[0], queries, jnp.concatenate(near))
    beside, last, running = lax.optimization_barrier((beside, last, running))
    beside_1 = swapped(beside, "core")
    heads = attention(1, plan, doc_lengths.shape[0], queries, jnp.concatenate(last), running)
    heads_beside = swapped(heads, "x")
    heads_1 = swapped(heads, "core")
    total = projected(heads, out_weight, x * NC + core, width, jnp.float32)
    total = projected(heads_1, weight_1, x * NC + core, width, jnp.float32, [total])
    heads_beside, total = lax.optimization_barrier((heads_beside, total))
    heads_beside_1 = swapped(heads_beside, "core")
    total = projected(heads_beside, beside, core, width, jnp.float32, [total])
    return projected(heads_beside_1, beside_1, core, width, jnp.bfloat16, [total])


def solution(mesh):
    fine = Mesh(mesh.devices.reshape(mesh.devices.shape[0], NY, NZ, NX, NC), ("dp", "y", "z", "x", "core"))
    rows, heads = ("dp", "y", "z"), ("x", "core")
    in_specs = (
        P(rows, heads),
        P(rows, heads),
        P(rows, heads),
        P(heads, None),
        P("dp"),
        P("dp"),
        P("dp", None),
        P("dp"),
    )
    return jax.shard_map(per_device, mesh=fine, in_specs=in_specs, out_specs=P(rows, heads), check_vma=False)
```

```python
import functools
import math

import jax
import jax.numpy as jnp
from jax import lax
from jax.experimental import pallas as pl
from jax.experimental.pallas import tpu as pltpu
from jax.sharding import Mesh
from jax.sharding import PartitionSpec as P

HEAD_WIDTH = 128
BLK = 128
NY, NZ, NX, NC = 4, 8, 2, 2
RANKS = NY * NZ
SLOTS = 2 * RANKS
CENTRES = ((0, 0), (0, 4), (2, 2), (2, -2))
STEPS = ((1, 0), (-1, 0), (0, 1), (0, -1))
PICKS = (((3, 0), (4, 0), (1, 0)), ((4, 1), (3, 0), (2, 1)), ((1, 1), (2, 1), (3, 0)), ((2, 0), (1, 1), (4, 0)))


def offsets():
    near = [[(cy + sy, cz + sz) for cy, cz in CENTRES] for sy, sz in ((0, 0), *STEPS)]
    last = [(near[n][m][0] + sy, near[n][m][1] + sz) for (sy, sz), picks in zip(STEPS, PICKS) for n, m in picks]
    every = [(dy % NY, dz % NZ) for dy, dz in [o for group in near for o in group] + last]
    assert sorted(every) == [(dy, dz) for dy in range(NY) for dz in range(NZ)]
    return every


NEAR = 20


MASKED = -1e30
LOWEST = -1e20


def moved(x, dy, dz):
    route = [(((i // NZ + dy) % NY) * NZ + (i % NZ + dz) % NZ, i) for i in range(RANKS)]
    return lax.ppermute(x, ("y", "z"), route)


def first_round(kv):
    return jnp.concatenate([kv] + [moved(kv, *c) for c in CENTRES[1:]])


def second_round(centres):
    return [centres] + [moved(centres, *s) for s in STEPS]


def third_round(near, rows):
    return [
        moved(jnp.concatenate([near[n][m * rows : (m + 1) * rows] for n, m in picks]), *step)
        for step, picks in zip(STEPS, PICKS)
    ]


COUNTS, OWN, ENDS, LISTS = 0, 4, 16, 64
CHUNK = 2
LONGEST = SLOTS + 2 * CHUNK


def listed(l, which, at):
    return LISTS + (2 * l + which) * LONGEST + at


def cosets_rank(y, z, dy, dz):
    return jnp.bitwise_and(y + dy, NY - 1) * NZ + jnp.bitwise_and(z + dz, NZ - 1)


def plan_kernel(order, lengths, reveal, step, plan):
    y, z = lax.axis_index("y"), lax.axis_index("z")
    now = step[0]
    own, low, high = [], [], []
    for t in range(2):
        block = order[2 * (y * NZ + z) + t]
        first, last = block * BLK, block * BLK + BLK - 1
        begin = jnp.int32(0)
        low_t, high_t = jnp.int32(0), jnp.int32(0)
        for d in range(lengths.shape[0]):
            end = begin + lengths[d]
            plan[ENDS + d] = end
            low_t = jnp.where((begin <= first) & (first < end), begin, low_t)
            high_t = jnp.where((begin <= last) & (last < end), end, high_t)
            begin = end
        plan[OWN + t] = block
        own.append(block)
        low.append(low_t)
        high.append(high_t)
    n = [jnp.int32(0)] * 4
    for i, (dy, dz) in enumerate(offsets()):
        rank = cosets_rank(y, z, dy, dz)
        stage = int(i >= NEAR)
        for e in range(2):
            key_block = order[2 * rank + e]
            row = (i - stage * NEAR) * (4 * BLK) + e * BLK
            begin = key_block * BLK
            for t in range(2):
                l = 2 * stage + t
                seen = (begin < high[t]) & (begin + BLK > low[t]) & (reveal[own[t], key_block] <= now)
                plan[listed(l, 0, n[l])] = row
                plan[listed(l, 1, n[l])] = key_block
                n[l] = n[l] + seen.astype(jnp.int32)
    for l in range(4):
        for i in range(2 * CHUNK - 1):
            plan[listed(l, 0, n[l] + i)] = 0
            plan[listed(l, 1, n[l] + i)] = SLOTS
        plan[COUNTS + l] = lax.div(n[l] + (CHUNK - 1), CHUNK)


def attention_kernel(plan, q_ref, kv, *refs, stage, docs):
    heads = q_ref.shape[1] // HEAD_WIDTH
    scale = math.log2(math.e) / math.sqrt(HEAD_WIDTH)
    if stage == 0:
        top_ref, total_ref, acc_ref, scores, probs = refs
    else:
        top_in, total_in, acc_in, out_ref, acc_ref, scores, probs = refs
    columns = heads * BLK

    for t in range(2):
        l = 2 * stage + t
        rows = pl.ds(t * BLK, BLK)
        q = jnp.concatenate([q_ref[rows, h * HEAD_WIDTH : (h + 1) * HEAD_WIDTH] for h in range(heads)])
        q = jnp.transpose(q)
        pos = plan[OWN + t] * BLK + lax.broadcasted_iota(jnp.int32, (1, BLK), 1)
        low, high = jnp.zeros((1, BLK), jnp.int32), jnp.zeros((1, BLK), jnp.int32)
        for d in reversed(range(docs)):
            high = jnp.where(pos < plan[ENDS + d], plan[ENDS + d], high)
        for d in range(docs):
            low = jnp.where(pos >= plan[ENDS + d], plan[ENDS + d], low)
        down = lax.broadcasted_iota(jnp.int32, (BLK, BLK), 0)
        if stage == 0:
            acc = acc_ref.at[t]
            acc[...] = jnp.zeros(acc.shape, jnp.float32)
            carry = jnp.full((1, columns), LOWEST, jnp.float32), jnp.zeros((8, columns), jnp.float32)
        else:
            acc = acc_ref
            acc[...] = acc_in[t]
            carry = top_in[t], total_in[t]

        def chunk_rows(i, start):
            return jnp.concatenate(
                [kv[pl.ds(pl.multiple_of(plan[listed(l, 0, CHUNK * i + e)] + start, BLK), BLK), :] for e in range(CHUNK)]
            )

        def score(i):
            s = jnp.dot(chunk_rows(i, 0), q, preferred_element_type=jnp.float32)
            for e in range(CHUNK):
                key = down + plan[listed(l, 1, CHUNK * i + e)] * BLK
                allowed = (key >= low) & (key < high)
                for h in range(heads):
                    part = s[e * BLK : (e + 1) * BLK, h * BLK : (h + 1) * BLK]
                    scores[i % 2, pl.ds(e * BLK, BLK), pl.ds(h * BLK, BLK)] = jnp.where(allowed, part, MASKED)

        def weigh(i, factor):
            acc[...] = acc[...] * factor + lax.dot_general(
                chunk_rows(jnp.maximum(i, 0), 2 * BLK),
                probs[...],
                (((0,), (0,)), ((), ())),
                preferred_element_type=jnp.float32,
            )

        def chunk(i, carry):
            top, total, factor = carry
            s = scores[i % 2]
            weigh(i - 1, factor)
            best = jnp.maximum(top, jnp.max(s, axis=0, keepdims=True))
            p = jnp.exp2(s * scale - best * scale)
            factor = jnp.exp2((top - best) * scale)
            probs[...] = p.astype(jnp.bfloat16)
            score(i + 1)
            return best, total * factor + jnp.sum(p.reshape(-1, 8, columns), axis=0), factor

        n = plan[COUNTS + l]
        score(0)
        probs[...] = jnp.zeros(probs.shape, jnp.bfloat16)
        top, total, factor = lax.fori_loop(0, n, chunk, (*carry, jnp.ones((1, columns), jnp.float32)))
        weigh(n - 1, factor)
        if stage == 0:
            top_ref[t] = top
            total_ref[t] = total
        else:
            out = acc[...] / jnp.sum(total, axis=0, keepdims=True)
            for h in range(heads):
                head = jnp.transpose(out[:, h * BLK : (h + 1) * BLK])
                out_ref[rows, h * HEAD_WIDTH : (h + 1) * HEAD_WIDTH] = head.astype(jnp.bfloat16)


SMEM = pl.BlockSpec(memory_space=pltpu.SMEM)
VMEM = pl.BlockSpec(memory_space=pltpu.VMEM)


def planned(block_order, doc_lengths, reveal_step, train_step):
    return pl.pallas_call(
        plan_kernel,
        out_shape=jax.ShapeDtypeStruct((listed(4, 0, 0),), jnp.int32),
        in_specs=[SMEM] * 4,
        out_specs=SMEM,
        name="plan",
    )(block_order, doc_lengths, reveal_step, train_step)


def attention(stage, plan, docs, queries, kv, before=()):
    columns = queries.shape[1] // HEAD_WIDTH * BLK
    running = [jax.ShapeDtypeStruct((2, r, columns), jnp.float32) for r in (1, 8, HEAD_WIDTH)]
    return pl.pallas_call(
        functools.partial(attention_kernel, stage=stage, docs=docs),
        out_shape=running if stage == 0 else jax.ShapeDtypeStruct(queries.shape, jnp.bfloat16),
        in_specs=[SMEM] + [VMEM] * (2 + len(before)),
        out_specs=[VMEM] * 3 if stage == 0 else VMEM,
        scratch_shapes=([] if stage == 0 else [pltpu.VMEM((HEAD_WIDTH, columns), jnp.float32)])
        + [
            pltpu.VMEM((2, CHUNK * BLK, columns), jnp.float32),
            pltpu.VMEM((CHUNK * BLK, columns), jnp.bfloat16),
        ],
        compiler_params=pltpu.CompilerParams(vmem_limit_bytes=7 * 2**20),
        cost_estimate=pl.CostEstimate(flops=10**9, bytes_accessed=10**7, transcendentals=3 * 10**6),
        name="attention_%d" % stage,
    )(plan, queries, kv, *before)


def swapped(x, axis):
    return lax.ppermute(x, axis, [(0, 1), (1, 0)])


def from_both_sides(x):
    ring = 2 * NX
    route = [(((i + (1, -1)[c]) % ring) * NC + c, i * NC + c) for i in range(ring) for c in range(NC)]
    return lax.ppermute(x, ("dp", "x", "core"), route)


def columns_of(weight, column, width):
    return lax.dynamic_slice_in_dim(weight, column * width, width, 1)


def project_kernel(heads, weight, *refs):
    *before, out_ref = refs
    total = jnp.dot(heads[...], weight[...], preferred_element_type=jnp.float32)
    if before:
        total = before[0][...] + total
    out_ref[...] = total.astype(out_ref.dtype)


def projected(heads, weight, dtype, before=()):
    rows, depth = heads.shape
    width = weight.shape[1]
    return pl.pallas_call(
        project_kernel,
        out_shape=jax.ShapeDtypeStruct((rows, width), dtype),
        in_specs=[VMEM] * (2 + len(before)),
        out_specs=VMEM,
        compiler_params=pltpu.CompilerParams(vmem_limit_bytes=6 * 2**20),
        cost_estimate=pl.CostEstimate(
            flops=2 * rows * width * depth, bytes_accessed=2 * width * depth, transcendentals=0
        ),
        name="project",
    )(heads, weight, *before)


def per_device(queries, keys, values, out_weight, block_order, doc_lengths, reveal_step, train_step):
    x, core = lax.axis_index("x"), lax.axis_index("core")
    width = out_weight.shape[1] // (NX * NC)
    rows = keys.shape[0]
    kv = jnp.where(
        lax.broadcasted_iota(jnp.int32, (2 * rows, 1), 0) < rows,
        jnp.pad(keys, ((0, rows), (0, 0))),
        jnp.pad(values, ((rows, 0), (0, 0))),
    )
    docs = doc_lengths.shape[0]
    beside = from_both_sides(columns_of(out_weight, 1 - x, NC * width))
    centres = first_round(kv)
    plan = planned(block_order, doc_lengths, reveal_step, train_step)
    weight_1 = swapped(out_weight, "core")
    centres, weight_1, plan = lax.optimization_barrier((centres, weight_1, plan))
    near = second_round(centres)
    own_columns = [columns_of(w, x * NC + core, width) for w in (out_weight, weight_1)]
    last = third_round(near, kv.shape[0])
    plan, *own_columns = lax.optimization_barrier((plan, *own_columns))
    running = attention(0, plan, docs, queries, jnp.concatenate(near))
    beside, last, running = lax.optimization_barrier((beside, last, running))
    beside_1 = swapped(beside, "core")
    heads = attention(1, plan, docs, queries, jnp.concatenate(last), running)
    heads_beside = swapped(heads, "x")
    heads_1 = swapped(heads, "core")
    total = projected(heads, own_columns[0], jnp.float32)
    total = projected(heads_1, own_columns[1], jnp.float32, [total])
    beside_columns = [columns_of(w, core, width) for w in (beside, beside_1)]
    heads_beside, total, *beside_columns = lax.optimization_barrier((heads_beside, total, *beside_columns))
    heads_beside_1 = swapped(heads_beside, "core")
    total = projected(heads_beside, beside_columns[0], jnp.float32, [total])
    return projected(heads_beside_1, beside_columns[1], jnp.bfloat16, [total])


def solution(mesh):
    fine = Mesh(mesh.devices.reshape(mesh.devices.shape[0], NY, NZ, NX, NC), ("dp", "y", "z", "x", "core"))
    rows, heads = ("dp", "y", "z"), ("x", "core")
    in_specs = (
        P(rows, heads),
        P(rows, heads),
        P(rows, heads),
        P(heads, None),
        P("dp"),
        P("dp"),
        P("dp", None),
        P("dp"),
    )
    return jax.shard_map(per_device, mesh=fine, in_specs=in_specs, out_specs=P(rows, heads), check_vma=False)
```

```python
import functools
import math

import jax
import jax.numpy as jnp
from jax import lax
from jax.experimental import pallas as pl
from jax.experimental.pallas import tpu as pltpu
from jax.sharding import Mesh
from jax.sharding import PartitionSpec as P

HEAD_WIDTH = 128
BLK = 128
NY, NZ, NX, NC = 4, 8, 2, 2
RANKS = NY * NZ
SLOTS = 2 * RANKS
CENTRES = ((0, 0), (0, 4), (2, 2), (2, -2))
STEPS = ((1, 0), (-1, 0), (0, 1), (0, -1))
PICKS = (((3, 0), (4, 0), (1, 0)), ((4, 1), (3, 0), (2, 1)), ((1, 1), (2, 1), (3, 0)), ((2, 0), (1, 1), (4, 0)))


def offsets():
    near = [[(cy + sy, cz + sz) for cy, cz in CENTRES] for sy, sz in ((0, 0), *STEPS)]
    last = [(near[n][m][0] + sy, near[n][m][1] + sz) for (sy, sz), picks in zip(STEPS, PICKS) for n, m in picks]
    every = [(dy % NY, dz % NZ) for dy, dz in [o for group in near for o in group] + last]
    assert sorted(every) == [(dy, dz) for dy in range(NY) for dz in range(NZ)]
    return every


NEAR = 20


MASKED = -1e30
LOWEST = -1e20


def moved(x, dy, dz):
    route = [(((i // NZ + dy) % NY) * NZ + (i % NZ + dz) % NZ, i) for i in range(RANKS)]
    return lax.ppermute(x, ("y", "z"), route)


def first_round(kv):
    return jnp.concatenate([kv] + [moved(kv, *c) for c in CENTRES[1:]])


def second_round(centres):
    return [centres] + [moved(centres, *s) for s in STEPS]


def third_round(near, rows):
    return [
        moved(jnp.concatenate([near[n][m * rows : (m + 1) * rows] for n, m in picks]), *step)
        for step, picks in zip(STEPS, PICKS)
    ]


COUNTS, OWN, ENDS, LISTS = 0, 4, 16, 64
CHUNK = 2
LONGEST = SLOTS + 2 * CHUNK


def listed(l, which, at):
    return LISTS + (2 * l + which) * LONGEST + at


def cosets_rank(y, z, dy, dz):
    return jnp.bitwise_and(y + dy, NY - 1) * NZ + jnp.bitwise_and(z + dz, NZ - 1)


def plan_kernel(order, lengths, reveal, step, plan):
    y, z = lax.axis_index("y"), lax.axis_index("z")
    now = step[0]
    own, low, high = [], [], []
    for t in range(2):
        block = order[2 * (y * NZ + z) + t]
        first, last = block * BLK, block * BLK + BLK - 1
        begin = jnp.int32(0)
        low_t, high_t = jnp.int32(0), jnp.int32(0)
        for d in range(lengths.shape[0]):
            end = begin + lengths[d]
            plan[ENDS + d] = end
            low_t = jnp.where((begin <= first) & (first < end), begin, low_t)
            high_t = jnp.where((begin <= last) & (last < end), end, high_t)
            begin = end
        plan[OWN + t] = block
        own.append(block)
        low.append(low_t)
        high.append(high_t)
    n = [jnp.int32(0)] * 4
    for i, (dy, dz) in enumerate(offsets()):
        rank = cosets_rank(y, z, dy, dz)
        stage = int(i >= NEAR)
        for e in range(2):
            key_block = order[2 * rank + e]
            row = (i - stage * NEAR) * (4 * BLK) + e * BLK
            begin = key_block * BLK
            for t in range(2):
                l = 2 * stage + t
                seen = (begin < high[t]) & (begin + BLK > low[t]) & (reveal[own[t], key_block] <= now)
                plan[listed(l, 0, n[l])] = row
                plan[listed(l, 1, n[l])] = key_block
                n[l] = n[l] + seen.astype(jnp.int32)
    for l in range(4):
        for i in range(2 * CHUNK - 1):
            plan[listed(l, 0, n[l] + i)] = 0
            plan[listed(l, 1, n[l] + i)] = SLOTS
        plan[COUNTS + l] = lax.div(n[l] + (CHUNK - 1), CHUNK)


def attention_kernel(plan, q_ref, kv, *refs, stage, docs):
    heads = q_ref.shape[1] // HEAD_WIDTH
    scale = math.log2(math.e) / math.sqrt(HEAD_WIDTH)
    if stage == 0:
        top_ref, total_ref, acc_ref, scores, probs = refs
    else:
        top_in, total_in, acc_in, out_ref, acc_ref, scores, probs = refs
    columns = heads * BLK

    for t in range(2):
        l = 2 * stage + t
        rows = pl.ds(t * BLK, BLK)
        q = jnp.concatenate([q_ref[rows, h * HEAD_WIDTH : (h + 1) * HEAD_WIDTH] for h in range(heads)])
        q = jnp.transpose(q)
        pos = plan[OWN + t] * BLK + lax.broadcasted_iota(jnp.int32, (1, BLK), 1)
        low, high = jnp.zeros((1, BLK), jnp.int32), jnp.zeros((1, BLK), jnp.int32)
        for d in reversed(range(docs)):
            high = jnp.where(pos < plan[ENDS + d], plan[ENDS + d], high)
        for d in range(docs):
            low = jnp.where(pos >= plan[ENDS + d], plan[ENDS + d], low)
        down = lax.broadcasted_iota(jnp.int32, (BLK, BLK), 0)
        if stage == 0:
            acc = acc_ref.at[t]
            acc[...] = jnp.zeros(acc.shape, jnp.float32)
            carry = jnp.full((1, columns), LOWEST, jnp.float32), jnp.zeros((8, columns), jnp.float32)
        else:
            acc = acc_ref
            acc[...] = acc_in[t]
            carry = top_in[t], total_in[t]

        def chunk_rows(i, start):
            return jnp.concatenate(
                [kv[pl.ds(pl.multiple_of(plan[listed(l, 0, CHUNK * i + e)] + start, BLK), BLK), :] for e in range(CHUNK)]
            )

        def score(i):
            s = jnp.dot(chunk_rows(i, 0), q, preferred_element_type=jnp.float32)
            for e in range(CHUNK):
                key = down + plan[listed(l, 1, CHUNK * i + e)] * BLK
                allowed = (key >= low) & (key < high)
                for h in range(heads):
                    part = s[e * BLK : (e + 1) * BLK, h * BLK : (h + 1) * BLK]
                    scores[i % 2, pl.ds(e * BLK, BLK), pl.ds(h * BLK, BLK)] = jnp.where(allowed, part, MASKED)

        def weigh(i, factor):
            acc[...] = acc[...] * factor + lax.dot_general(
                chunk_rows(jnp.maximum(i, 0), 2 * BLK),
                probs[...],
                (((0,), (0,)), ((), ())),
                preferred_element_type=jnp.float32,
            )

        def chunk(i, carry):
            top, total, factor = carry
            s = scores[i % 2]
            weigh(i - 1, factor)
            best = jnp.maximum(top, jnp.max(s, axis=0, keepdims=True))
            p = jnp.exp2(s * scale - best * scale)
            factor = jnp.exp2((top - best) * scale)
            probs[...] = p.astype(jnp.bfloat16)
            score(i + 1)
            return best, total * factor + jnp.sum(p.reshape(-1, 8, columns), axis=0), factor

        n = plan[COUNTS + l]
        score(0)
        probs[...] = jnp.zeros(probs.shape, jnp.bfloat16)
        top, total, factor = lax.fori_loop(0, n, chunk, (*carry, jnp.ones((1, columns), jnp.float32)))
        weigh(n - 1, factor)
        if stage == 0:
            top_ref[t] = top
            total_ref[t] = total
        else:
            out = acc[...] / jnp.sum(total, axis=0, keepdims=True)
            for h in range(heads):
                head = jnp.transpose(out[:, h * BLK : (h + 1) * BLK])
                out_ref[rows, h * HEAD_WIDTH : (h + 1) * HEAD_WIDTH] = head.astype(jnp.bfloat16)


SMEM = pl.BlockSpec(memory_space=pltpu.SMEM)
VMEM = pl.BlockSpec(memory_space=pltpu.VMEM)


def planned(block_order, doc_lengths, reveal_step, train_step):
    return pl.pallas_call(
        plan_kernel,
        out_shape=jax.ShapeDtypeStruct((listed(4, 0, 0),), jnp.int32),
        in_specs=[SMEM] * 4,
        out_specs=SMEM,
        name="plan",
    )(block_order, doc_lengths, reveal_step, train_step)


def attention(stage, plan, docs, queries, kv, before=()):
    columns = queries.shape[1] // HEAD_WIDTH * BLK
    running = [jax.ShapeDtypeStruct((2, r, columns), jnp.float32) for r in (1, 8, HEAD_WIDTH)]
    return pl.pallas_call(
        functools.partial(attention_kernel, stage=stage, docs=docs),
        out_shape=running if stage == 0 else jax.ShapeDtypeStruct(queries.shape, jnp.bfloat16),
        in_specs=[SMEM] + [VMEM] * (2 + len(before)),
        out_specs=[VMEM] * 3 if stage == 0 else VMEM,
        scratch_shapes=([] if stage == 0 else [pltpu.VMEM((HEAD_WIDTH, columns), jnp.float32)])
        + [
            pltpu.VMEM((2, CHUNK * BLK, columns), jnp.float32),
            pltpu.VMEM((CHUNK * BLK, columns), jnp.bfloat16),
        ],
        compiler_params=pltpu.CompilerParams(vmem_limit_bytes=7 * 2**20),
        cost_estimate=pl.CostEstimate(flops=10**9, bytes_accessed=10**7, transcendentals=3 * 10**6),
        name="attention_%d" % stage,
    )(plan, queries, kv, *before)


def swapped(x, axis):
    return lax.ppermute(x, axis, [(0, 1), (1, 0)])


def from_both_sides(x):
    ring = 2 * NX
    route = [(((i + (1, -1)[c]) % ring) * NC + c, i * NC + c) for i in range(ring) for c in range(NC)]
    return lax.ppermute(x, ("dp", "x", "core"), route)


def columns_of(weight, column, width):
    return lax.dynamic_slice_in_dim(weight, column * width, width, 1)


def project_kernel(heads, weight, *refs):
    *before, out_ref = refs
    total = jnp.dot(heads[...], weight[...], preferred_element_type=jnp.float32)
    if before:
        total = before[0][...] + total
    out_ref[...] = total.astype(out_ref.dtype)


def projected(heads, weight, dtype, before=()):
    rows, depth = heads.shape
    width = weight.shape[1]
    return pl.pallas_call(
        project_kernel,
        out_shape=jax.ShapeDtypeStruct((rows, width), dtype),
        in_specs=[VMEM] * (2 + len(before)),
        out_specs=VMEM,
        compiler_params=pltpu.CompilerParams(vmem_limit_bytes=6 * 2**20),
        cost_estimate=pl.CostEstimate(
            flops=2 * rows * width * depth, bytes_accessed=2 * width * depth, transcendentals=0
        ),
        name="project",
    )(heads, weight, *before)


def per_device(queries, keys, values, out_weight, block_order, doc_lengths, reveal_step, train_step):
    x, core = lax.axis_index("x"), lax.axis_index("core")
    width = out_weight.shape[1] // (NX * NC)
    rows = keys.shape[0]
    kv = jnp.where(
        lax.broadcasted_iota(jnp.int32, (2 * rows, 1), 0) < rows,
        jnp.pad(keys, ((0, rows), (0, 0))),
        jnp.pad(values, ((rows, 0), (0, 0))),
    )
    docs = doc_lengths.shape[0]
    beside = from_both_sides(columns_of(out_weight, 1 - x, NC * width))
    centres = first_round(kv)
    plan = planned(block_order, doc_lengths, reveal_step, train_step)
    weight_1 = swapped(out_weight, "core")
    centres, weight_1, plan, late_weight = lax.optimization_barrier((centres, weight_1, plan, out_weight))
    near = second_round(centres)
    own_columns = [columns_of(w, x * NC + core, width) for w in (late_weight, weight_1)]
    last = third_round(near, kv.shape[0])
    plan, *own_columns = lax.optimization_barrier((plan, *own_columns))
    running = attention(0, plan, docs, queries, jnp.concatenate(near))
    heads = attention(1, plan, docs, queries, jnp.concatenate(last), running)
    beside, after = lax.optimization_barrier((beside, heads))
    beside_1 = swapped(beside, "core")
    heads_beside = swapped(heads, "x")
    heads_1 = swapped(heads, "core")
    total = projected(heads, own_columns[0], jnp.float32)
    total = projected(heads_1, own_columns[1], jnp.float32, [total])
    beside_columns = [columns_of(w, core, width) for w in (beside, beside_1)]
    heads_beside, total, *beside_columns = lax.optimization_barrier((heads_beside, total, *beside_columns))
    heads_beside_1 = swapped(heads_beside, "core")
    total = projected(heads_beside, beside_columns[0], jnp.float32, [total])
    return projected(heads_beside_1, beside_columns[1], jnp.bfloat16, [total])


def solution(mesh):
    fine = Mesh(mesh.devices.reshape(mesh.devices.shape[0], NY, NZ, NX, NC), ("dp", "y", "z", "x", "core"))
    rows, heads = ("dp", "y", "z"), ("x", "core")
    in_specs = (
        P(rows, heads),
        P(rows, heads),
        P(rows, heads),
        P(heads, None),
        P("dp"),
        P("dp"),
        P("dp", None),
        P("dp"),
    )
    return jax.shard_map(per_device, mesh=fine, in_specs=in_specs, out_specs=P(rows, heads), check_vma=False)
```

```python
import functools
import math

import jax
import jax.numpy as jnp
from jax import lax
from jax.experimental import pallas as pl
from jax.experimental.pallas import tpu as pltpu
from jax.sharding import Mesh
from jax.sharding import PartitionSpec as P

HEAD_WIDTH = 128
BLK = 128
NY, NZ, NX, NC = 4, 8, 2, 2
RANKS = NY * NZ
SLOTS = 2 * RANKS
CENTRES = ((0, 0), (2, 2), (2, -2), (0, 4))
STEPS = ((0, 1), (0, -1), (1, 0), (-1, 0))
PICKS = (((3, 3), (4, 3), (1, 0)), ((4, 0), (3, 3), (2, 0)), ((1, 0), (2, 0), (3, 0)), ((2, 3), (1, 0), (4, 3)))


def offsets():
    near = [[(cy + sy, cz + sz) for cy, cz in CENTRES] for sy, sz in ((0, 0), *STEPS)]
    last = [(near[n][m][0] + sy, near[n][m][1] + sz) for (sy, sz), picks in zip(STEPS, PICKS) for n, m in picks]
    every = [(dy % NY, dz % NZ) for dy, dz in [o for group in near for o in group] + last]
    assert sorted(every) == [(dy, dz) for dy in range(NY) for dz in range(NZ)]
    return every


NEAR = 20


MASKED = -1e30
LOWEST = -1e20


def moved(x, dy, dz):
    route = [(((i // NZ + dy) % NY) * NZ + (i % NZ + dz) % NZ, i) for i in range(RANKS)]
    return lax.ppermute(x, ("y", "z"), route)


def first_round(kv):
    return jnp.concatenate([kv] + [moved(kv, *c) for c in CENTRES[1:]])


def second_round(centres):
    return [centres] + [moved(centres, *s) for s in STEPS]


def third_round(near, rows):
    return [
        moved(jnp.concatenate([near[n][m * rows : (m + 1) * rows] for n, m in picks]), *step)
        for step, picks in zip(STEPS, PICKS)
    ]


COUNTS, OWN, ENDS, LISTS = 0, 4, 16, 64
CHUNK = 2
LONGEST = SLOTS + 2 * CHUNK


def listed(l, which, at):
    return LISTS + (2 * l + which) * LONGEST + at


def cosets_rank(y, z, dy, dz):
    return jnp.bitwise_and(y + dy, NY - 1) * NZ + jnp.bitwise_and(z + dz, NZ - 1)


def plan_kernel(order, lengths, reveal, step, plan):
    y, z = lax.axis_index("y"), lax.axis_index("z")
    now = step[0]
    own, low, high = [], [], []
    for t in range(2):
        block = order[2 * (y * NZ + z) + t]
        first, last = block * BLK, block * BLK + BLK - 1
        begin = jnp.int32(0)
        low_t, high_t = jnp.int32(0), jnp.int32(0)
        for d in range(lengths.shape[0]):
            end = begin + lengths[d]
            plan[ENDS + d] = end
            low_t = jnp.where((begin <= first) & (first < end), begin, low_t)
            high_t = jnp.where((begin <= last) & (last < end), end, high_t)
            begin = end
        plan[OWN + t] = block
        own.append(block)
        low.append(low_t)
        high.append(high_t)
    n = [jnp.int32(0)] * 4
    for i, (dy, dz) in enumerate(offsets()):
        rank = cosets_rank(y, z, dy, dz)
        stage = int(i >= NEAR)
        for e in range(2):
            key_block = order[2 * rank + e]
            row = (i - stage * NEAR) * (4 * BLK) + e * BLK
            begin = key_block * BLK
            for t in range(2):
                l = 2 * stage + t
                seen = (begin < high[t]) & (begin + BLK > low[t]) & (reveal[own[t], key_block] <= now)
                plan[listed(l, 0, n[l])] = row
                plan[listed(l, 1, n[l])] = key_block
                n[l] = n[l] + seen.astype(jnp.int32)
    for l in range(4):
        for i in range(2 * CHUNK - 1):
            plan[listed(l, 0, n[l] + i)] = 0
            plan[listed(l, 1, n[l] + i)] = SLOTS
        plan[COUNTS + l] = lax.div(n[l] + (CHUNK - 1), CHUNK)


def attention_kernel(plan, q_ref, kv, *refs, stage, docs):
    heads = q_ref.shape[1] // HEAD_WIDTH
    scale = math.log2(math.e) / math.sqrt(HEAD_WIDTH)
    if stage == 0:
        top_ref, total_ref, acc_ref, scores, probs = refs
    else:
        top_in, total_in, acc_in, out_ref, acc_ref, scores, probs = refs
    columns = heads * BLK

    down = lax.broadcasted_iota(jnp.int32, (BLK, BLK), 0)
    queries, bounds, start, n = [], [], [], []
    for t in range(2):
        rows = pl.ds(t * BLK, BLK)
        q = jnp.concatenate([q_ref[rows, h * HEAD_WIDTH : (h + 1) * HEAD_WIDTH] for h in range(heads)])
        queries.append(jnp.transpose(q))
        pos = plan[OWN + t] * BLK + lax.broadcasted_iota(jnp.int32, (1, BLK), 1)
        low, high = jnp.zeros((1, BLK), jnp.int32), jnp.zeros((1, BLK), jnp.int32)
        for d in reversed(range(docs)):
            high = jnp.where(pos < plan[ENDS + d], plan[ENDS + d], high)
        for d in range(docs):
            low = jnp.where(pos >= plan[ENDS + d], plan[ENDS + d], low)
        bounds.append((low, high))
        if stage == 0:
            acc_ref[t] = jnp.zeros(acc_ref.shape[1:], jnp.float32)
            first = jnp.full((1, columns), LOWEST, jnp.float32), jnp.zeros((8, columns), jnp.float32)
        else:
            acc_ref[t] = acc_in[t]
            first = top_in[t], total_in[t]
        start.append((*first, jnp.ones((1, columns), jnp.float32)))
        n.append(plan[COUNTS + 2 * stage + t])

    def chunk_rows(t, i, after):
        l = 2 * stage + t
        at = [plan[listed(l, 0, CHUNK * i + e)] + after for e in range(CHUNK)]
        return jnp.concatenate([kv[pl.ds(pl.multiple_of(a, BLK), BLK), :] for a in at])

    def score(t, i):
        s = jnp.dot(chunk_rows(t, i, 0), queries[t], preferred_element_type=jnp.float32)
        low, high = bounds[t]
        for e in range(CHUNK):
            key = down + plan[listed(2 * stage + t, 1, CHUNK * i + e)] * BLK
            allowed = (key >= low) & (key < high)
            for h in range(heads):
                part = s[e * BLK : (e + 1) * BLK, h * BLK : (h + 1) * BLK]
                scores[t, i % 2, pl.ds(e * BLK, BLK), pl.ds(h * BLK, BLK)] = jnp.where(allowed, part, MASKED)

    def weigh(t, i, factor):
        j = jnp.maximum(i, 0)
        acc_ref[t] = acc_ref[t] * factor + lax.dot_general(
            chunk_rows(t, j, 2 * BLK), probs[t], (((0,), (0,)), ((), ())), preferred_element_type=jnp.float32
        )

    def chunk(t, i, carry):
        top, total, factor = carry
        s = scores[t, i % 2]
        weigh(t, i - 1, factor)
        best = jnp.maximum(top, jnp.max(s, axis=0, keepdims=True))
        p = jnp.exp2(s * scale - best * scale)
        factor = jnp.exp2((top - best) * scale)
        probs[t] = p.astype(jnp.bfloat16)
        score(t, i + 1)
        return best, total * factor + jnp.sum(p.reshape(-1, 8, columns), axis=0), factor

    for t in range(2):
        score(t, 0)
        probs[t] = jnp.zeros(probs.shape[1:], jnp.bfloat16)
    end = [lax.fori_loop(0, n[t], functools.partial(chunk, t), start[t]) for t in range(2)]
    for t in range(2):
        top, total, factor = end[t]
        weigh(t, n[t] - 1, factor)
        if stage == 0:
            top_ref[t] = top
            total_ref[t] = total
        else:
            out = acc_ref[t] / jnp.sum(total, axis=0, keepdims=True)
            for h in range(heads):
                head = jnp.transpose(out[:, h * BLK : (h + 1) * BLK])
                out_ref[t * BLK : (t + 1) * BLK, h * HEAD_WIDTH : (h + 1) * HEAD_WIDTH] = head.astype(jnp.bfloat16)


SMEM = pl.BlockSpec(memory_space=pltpu.SMEM)
VMEM = pl.BlockSpec(memory_space=pltpu.VMEM)


def planned(block_order, doc_lengths, reveal_step, train_step):
    return pl.pallas_call(
        plan_kernel,
        out_shape=jax.ShapeDtypeStruct((listed(4, 0, 0),), jnp.int32),
        in_specs=[SMEM] * 4,
        out_specs=SMEM,
        name="plan",
    )(block_order, doc_lengths, reveal_step, train_step)


def attention(stage, plan, docs, queries, kv, before=()):
    columns = queries.shape[1] // HEAD_WIDTH * BLK
    running = [jax.ShapeDtypeStruct((2, r, columns), jnp.float32) for r in (1, 8, HEAD_WIDTH)]
    return pl.pallas_call(
        functools.partial(attention_kernel, stage=stage, docs=docs),
        out_shape=running if stage == 0 else jax.ShapeDtypeStruct(queries.shape, jnp.bfloat16),
        in_specs=[SMEM] + [VMEM] * (2 + len(before)),
        out_specs=[VMEM] * 3 if stage == 0 else VMEM,
        scratch_shapes=([] if stage == 0 else [pltpu.VMEM((2, HEAD_WIDTH, columns), jnp.float32)])
        + [
            pltpu.VMEM((2, 2, CHUNK * BLK, columns), jnp.float32),
            pltpu.VMEM((2, CHUNK * BLK, columns), jnp.bfloat16),
        ],
        compiler_params=pltpu.CompilerParams(vmem_limit_bytes=9 * 2**20),
        cost_estimate=pl.CostEstimate(flops=10**9, bytes_accessed=10**7, transcendentals=3 * 10**6),
        name="attention_%d" % stage,
    )(plan, queries, kv, *before)


def swapped(x, axis):
    return lax.ppermute(x, axis, [(0, 1), (1, 0)])


def from_both_sides(x):
    ring = 2 * NX
    route = [(((i + (1, -1)[c]) % ring) * NC + c, i * NC + c) for i in range(ring) for c in range(NC)]
    return lax.ppermute(x, ("dp", "x", "core"), route)


def columns_of(weight, column, width):
    return lax.dynamic_slice_in_dim(weight, column * width, width, 1)


def project_kernel(heads, weight, *refs):
    *before, out_ref = refs
    total = jnp.dot(heads[...], weight[...], preferred_element_type=jnp.float32)
    if before:
        total = before[0][...] + total
    out_ref[...] = total.astype(out_ref.dtype)


def projected(heads, weight, dtype, before=()):
    rows, depth = heads.shape
    width = weight.shape[1]
    return pl.pallas_call(
        project_kernel,
        out_shape=jax.ShapeDtypeStruct((rows, width), dtype),
        in_specs=[VMEM] * (2 + len(before)),
        out_specs=VMEM,
        compiler_params=pltpu.CompilerParams(vmem_limit_bytes=6 * 2**20),
        cost_estimate=pl.CostEstimate(
            flops=2 * rows * width * depth, bytes_accessed=2 * width * depth, transcendentals=0
        ),
        name="project",
    )(heads, weight, *before)


def per_device(queries, keys, values, out_weight, block_order, doc_lengths, reveal_step, train_step):
    x, core = lax.axis_index("x"), lax.axis_index("core")
    width = out_weight.shape[1] // (NX * NC)
    rows = keys.shape[0]
    kv = jnp.where(
        lax.broadcasted_iota(jnp.int32, (2 * rows, 1), 0) < rows,
        jnp.pad(keys, ((0, rows), (0, 0))),
        jnp.pad(values, ((rows, 0), (0, 0))),
    )
    docs = doc_lengths.shape[0]
    beside = from_both_sides(columns_of(out_weight, 1 - x, NC * width))
    centres = first_round(kv)
    plan = planned(block_order, doc_lengths, reveal_step, train_step)
    weight_1 = swapped(out_weight, "core")
    centres, weight_1, plan, late_weight = lax.optimization_barrier((centres, weight_1, plan, out_weight))
    near = second_round(centres)
    own_columns = [columns_of(w, x * NC + core, width) for w in (late_weight, weight_1)]
    last = third_round(near, kv.shape[0])
    plan, *own_columns = lax.optimization_barrier((plan, *own_columns))
    running = attention(0, plan, docs, queries, jnp.concatenate(near))
    heads = attention(1, plan, docs, queries, jnp.concatenate(last), running)
    beside, after = lax.optimization_barrier((beside, heads))
    beside_1 = swapped(beside, "core")
    heads_beside = swapped(heads, "x")
    heads_1 = swapped(heads, "core")
    total = projected(heads, own_columns[0], jnp.float32)
    total = projected(heads_1, own_columns[1], jnp.float32, [total])
    beside_columns = [columns_of(w, core, width) for w in (beside, beside_1)]
    heads_beside, total, *beside_columns = lax.optimization_barrier((heads_beside, total, *beside_columns))
    heads_beside_1 = swapped(heads_beside, "core")
    total = projected(heads_beside, beside_columns[0], jnp.float32, [total])
    return projected(heads_beside_1, beside_columns[1], jnp.bfloat16, [total])


def solution(mesh):
    fine = Mesh(mesh.devices.reshape(mesh.devices.shape[0], NY, NZ, NX, NC), ("dp", "y", "z", "x", "core"))
    rows, heads = ("dp", "y", "z"), ("x", "core")
    in_specs = (
        P(rows, heads),
        P(rows, heads),
        P(rows, heads),
        P(heads, None),
        P("dp"),
        P("dp"),
        P("dp", None),
        P("dp"),
    )
    return jax.shard_map(per_device, mesh=fine, in_specs=in_specs, out_specs=P(rows, heads), check_vma=False)
```

```python
import functools
import math

import jax
import jax.numpy as jnp
from jax import lax
from jax.experimental import pallas as pl
from jax.experimental.pallas import tpu as pltpu
from jax.sharding import Mesh
from jax.sharding import PartitionSpec as P

HEAD_WIDTH = 128
BLK = 128
NY, NZ, NX, NC = 4, 8, 2, 2
RANKS = NY * NZ
SLOTS = 2 * RANKS
CENTRES = ((0, 0), (2, 2), (2, -2), (0, 4))
STEPS = ((0, 1), (0, -1), (1, 0), (-1, 0))
PICKS = (((3, 3), (4, 3), (1, 0)), ((4, 0), (3, 3), (2, 0)), ((1, 0), (2, 0), (3, 0)), ((2, 3), (1, 0), (4, 3)))


def offsets():
    near = [[(cy + sy, cz + sz) for cy, cz in CENTRES] for sy, sz in ((0, 0), *STEPS)]
    last = [(near[n][m][0] + sy, near[n][m][1] + sz) for (sy, sz), picks in zip(STEPS, PICKS) for n, m in picks]
    every = [(dy % NY, dz % NZ) for dy, dz in [o for group in near for o in group] + last]
    assert sorted(every) == [(dy, dz) for dy in range(NY) for dz in range(NZ)]
    return every


NEAR = 20


MASKED = -1e30
LOWEST = -1e20


def moved(x, dy, dz):
    route = [(((i // NZ + dy) % NY) * NZ + (i % NZ + dz) % NZ, i) for i in range(RANKS)]
    return lax.ppermute(x, ("y", "z"), route)


def first_round(kv):
    return jnp.concatenate([kv] + [moved(kv, *c) for c in CENTRES[1:]])


def second_round(centres):
    return [centres] + [moved(centres, *s) for s in STEPS]


def third_round(near, rows):
    return [
        moved(jnp.concatenate([near[n][m * rows : (m + 1) * rows] for n, m in picks]), *step)
        for step, picks in zip(STEPS, PICKS)
    ]


COUNTS, OWN, ENDS, LISTS = 0, 4, 16, 64
CHUNK = 2
LONGEST = SLOTS + 2 * CHUNK


def listed(l, which, at):
    return LISTS + (2 * l + which) * LONGEST + at


def cosets_rank(y, z, dy, dz):
    return jnp.bitwise_and(y + dy, NY - 1) * NZ + jnp.bitwise_and(z + dz, NZ - 1)


def plan_kernel(order, lengths, reveal, step, plan):
    y, z = lax.axis_index("y"), lax.axis_index("z")
    now = step[0]
    own, low, high = [], [], []
    for t in range(2):
        block = order[2 * (y * NZ + z) + t]
        first, last = block * BLK, block * BLK + BLK - 1
        begin = jnp.int32(0)
        low_t, high_t = jnp.int32(0), jnp.int32(0)
        for d in range(lengths.shape[0]):
            end = begin + lengths[d]
            plan[ENDS + d] = end
            low_t = jnp.where((begin <= first) & (first < end), begin, low_t)
            high_t = jnp.where((begin <= last) & (last < end), end, high_t)
            begin = end
        plan[OWN + t] = block
        own.append(block)
        low.append(low_t)
        high.append(high_t)
    n = [jnp.int32(0)] * 4
    for i, (dy, dz) in enumerate(offsets()):
        rank = cosets_rank(y, z, dy, dz)
        stage = int(i >= NEAR)
        for e in range(2):
            key_block = order[2 * rank + e]
            row = (i - stage * NEAR) * (4 * BLK) + e * BLK
            begin = key_block * BLK
            for t in range(2):
                l = 2 * stage + t
                seen = (begin < high[t]) & (begin + BLK > low[t]) & (reveal[own[t], key_block] <= now)
                plan[listed(l, 0, n[l])] = row
                plan[listed(l, 1, n[l])] = key_block
                n[l] = n[l] + seen.astype(jnp.int32)
    for l in range(4):
        for i in range(2 * CHUNK - 1):
            plan[listed(l, 0, n[l] + i)] = 0
            plan[listed(l, 1, n[l] + i)] = SLOTS
        plan[COUNTS + l] = lax.div(n[l] + (CHUNK - 1), CHUNK)


def attention_kernel(plan, q_ref, kv, *refs, stage, docs):
    heads = q_ref.shape[1] // HEAD_WIDTH
    scale = math.log2(math.e) / math.sqrt(HEAD_WIDTH)
    if stage == 0:
        top_ref, total_ref, acc_ref, scores, probs = refs
    else:
        top_in, total_in, acc_in, out_ref, acc_ref, scores, probs = refs
    columns = heads * BLK

    down = lax.broadcasted_iota(jnp.int32, (BLK, BLK), 0)
    queries, bounds, start, n = [], [], [], []
    for t in range(2):
        rows = pl.ds(t * BLK, BLK)
        q = jnp.concatenate([q_ref[rows, h * HEAD_WIDTH : (h + 1) * HEAD_WIDTH] for h in range(heads)])
        queries.append(jnp.transpose(q))
        pos = plan[OWN + t] * BLK + lax.broadcasted_iota(jnp.int32, (1, BLK), 1)
        low, high = jnp.zeros((1, BLK), jnp.int32), jnp.zeros((1, BLK), jnp.int32)
        for d in reversed(range(docs)):
            high = jnp.where(pos < plan[ENDS + d], plan[ENDS + d], high)
        for d in range(docs):
            low = jnp.where(pos >= plan[ENDS + d], plan[ENDS + d], low)
        bounds.append((low, high))
        if stage == 0:
            acc_ref[t] = jnp.zeros(acc_ref.shape[1:], jnp.float32)
            first = jnp.full((1, columns), LOWEST, jnp.float32), jnp.zeros((8, columns), jnp.float32)
        else:
            acc_ref[t] = acc_in[t]
            first = top_in[t], total_in[t]
        start.append((*first, jnp.ones((1, columns), jnp.float32)))
        n.append(plan[COUNTS + 2 * stage + t])

    def chunk_rows(t, i, after):
        l = 2 * stage + t
        at = [plan[listed(l, 0, CHUNK * i + e)] + after for e in range(CHUNK)]
        return jnp.concatenate([kv[pl.ds(pl.multiple_of(a, BLK), BLK), :] for a in at])

    def score(t, i):
        s = jnp.dot(chunk_rows(t, i, 0), queries[t], preferred_element_type=jnp.float32)
        low, high = bounds[t]
        for e in range(CHUNK):
            key = down + plan[listed(2 * stage + t, 1, CHUNK * i + e)] * BLK
            allowed = (key >= low) & (key < high)
            for h in range(heads):
                part = s[e * BLK : (e + 1) * BLK, h * BLK : (h + 1) * BLK]
                scores[t, i % 2, pl.ds(e * BLK, BLK), pl.ds(h * BLK, BLK)] = jnp.where(allowed, part, MASKED)

    def weigh(t, i, factor):
        j = jnp.maximum(i, 0)
        acc_ref[t] = acc_ref[t] * factor + lax.dot_general(
            chunk_rows(t, j, 2 * BLK), probs[t], (((0,), (0,)), ((), ())), preferred_element_type=jnp.float32
        )

    def chunk(t, i, carry):
        top, total, factor = carry
        s = scores[t, i % 2]
        weigh(t, i - 1, factor)
        best = jnp.maximum(top, jnp.max(s, axis=0, keepdims=True))
        p = jnp.exp2(s * scale - best * scale)
        factor = jnp.exp2((top - best) * scale)
        probs[t] = p.astype(jnp.bfloat16)
        score(t, i + 1)
        return best, total * factor + jnp.sum(p.reshape(-1, 8, columns), axis=0), factor

    for t in range(2):
        score(t, 0)
        probs[t] = jnp.zeros(probs.shape[1:], jnp.bfloat16)
    end = [lax.fori_loop(0, n[t], functools.partial(chunk, t), start[t]) for t in range(2)]
    for t in range(2):
        top, total, factor = end[t]
        weigh(t, n[t] - 1, factor)
        if stage == 0:
            top_ref[t] = top
            total_ref[t] = total
        else:
            out = acc_ref[t] / jnp.sum(total, axis=0, keepdims=True)
            for h in range(heads):
                head = jnp.transpose(out[:, h * BLK : (h + 1) * BLK])
                out_ref[t * BLK : (t + 1) * BLK, h * HEAD_WIDTH : (h + 1) * HEAD_WIDTH] = head.astype(jnp.bfloat16)


SMEM = pl.BlockSpec(memory_space=pltpu.SMEM)
VMEM = pl.BlockSpec(memory_space=pltpu.VMEM)


def planned(block_order, doc_lengths, reveal_step, train_step):
    return pl.pallas_call(
        plan_kernel,
        out_shape=jax.ShapeDtypeStruct((listed(4, 0, 0),), jnp.int32),
        in_specs=[SMEM] * 4,
        out_specs=SMEM,
        name="plan",
    )(block_order, doc_lengths, reveal_step, train_step)


def attention(stage, plan, docs, queries, kv, before=()):
    columns = queries.shape[1] // HEAD_WIDTH * BLK
    running = [jax.ShapeDtypeStruct((2, r, columns), jnp.float32) for r in (1, 8, HEAD_WIDTH)]
    return pl.pallas_call(
        functools.partial(attention_kernel, stage=stage, docs=docs),
        out_shape=running if stage == 0 else jax.ShapeDtypeStruct(queries.shape, jnp.bfloat16),
        in_specs=[SMEM] + [VMEM] * (2 + len(before)),
        out_specs=[VMEM] * 3 if stage == 0 else VMEM,
        scratch_shapes=([] if stage == 0 else [pltpu.VMEM((2, HEAD_WIDTH, columns), jnp.float32)])
        + [
            pltpu.VMEM((2, 2, CHUNK * BLK, columns), jnp.float32),
            pltpu.VMEM((2, CHUNK * BLK, columns), jnp.bfloat16),
        ],
        compiler_params=pltpu.CompilerParams(vmem_limit_bytes=9 * 2**20),
        cost_estimate=pl.CostEstimate(flops=10**9, bytes_accessed=10**7, transcendentals=3 * 10**6),
        name="attention_%d" % stage,
    )(plan, queries, kv, *before)


def swapped(x, axis):
    return lax.ppermute(x, axis, [(0, 1), (1, 0)])


def from_both_sides(x):
    ring = 2 * NX
    route = [(((i + (1, -1)[c]) % ring) * NC + c, i * NC + c) for i in range(ring) for c in range(NC)]
    return lax.ppermute(x, ("dp", "x", "core"), route)


def columns_of(weight, column, width):
    return lax.dynamic_slice_in_dim(weight, column * width, width, 1)


def project_kernel(heads, weight, *refs):
    *before, out_ref = refs
    total = jnp.dot(heads[...], weight[...], preferred_element_type=jnp.float32)
    if before:
        total = before[0][...] + total
    out_ref[...] = total.astype(out_ref.dtype)


def projected(heads, weight, dtype, before=()):
    rows, depth = heads.shape
    width = weight.shape[1]
    return pl.pallas_call(
        project_kernel,
        out_shape=jax.ShapeDtypeStruct((rows, width), dtype),
        in_specs=[VMEM] * (2 + len(before)),
        out_specs=VMEM,
        compiler_params=pltpu.CompilerParams(vmem_limit_bytes=6 * 2**20),
        cost_estimate=pl.CostEstimate(
            flops=2 * rows * width * depth, bytes_accessed=2 * width * depth, transcendentals=0
        ),
        name="project",
    )(heads, weight, *before)


def per_device(queries, keys, values, out_weight, block_order, doc_lengths, reveal_step, train_step):
    x, core = lax.axis_index("x"), lax.axis_index("core")
    width = out_weight.shape[1] // (NX * NC)
    rows = keys.shape[0]
    kv = jnp.where(
        lax.broadcasted_iota(jnp.int32, (2 * rows, 1), 0) < rows,
        jnp.pad(keys, ((0, rows), (0, 0))),
        jnp.pad(values, ((rows, 0), (0, 0))),
    )
    docs = doc_lengths.shape[0]
    beside = from_both_sides(columns_of(out_weight, 1 - x, NC * width))
    centres = first_round(kv)
    plan = planned(block_order, doc_lengths, reveal_step, train_step)
    weight_1 = swapped(out_weight, "core")
    centres, weight_1, plan, late_weight = lax.optimization_barrier((centres, weight_1, plan, out_weight))
    near = second_round(centres)
    own_columns = [columns_of(w, x * NC + core, width) for w in (late_weight, weight_1)]
    last = third_round(near, kv.shape[0])
    plan, *own_columns = lax.optimization_barrier((plan, *own_columns))
    running = attention(0, plan, docs, queries, jnp.concatenate(near))
    heads = attention(1, plan, docs, queries, jnp.concatenate(last), running)
    beside, after = lax.optimization_barrier((beside, heads))
    beside_1 = swapped(columns_of(beside, 1 - core, width), "core")
    heads_beside = swapped(heads, "x")
    heads_1 = swapped(heads, "core")
    total = projected(heads, own_columns[0], jnp.float32)
    total = projected(heads_1, own_columns[1], jnp.float32, [total])
    beside_columns = [columns_of(beside, core, width), beside_1]
    heads_beside, total, *beside_columns = lax.optimization_barrier((heads_beside, total, *beside_columns))
    heads_beside_1 = swapped(heads_beside, "core")
    total = projected(heads_beside, beside_columns[0], jnp.float32, [total])
    return projected(heads_beside_1, beside_columns[1], jnp.bfloat16, [total])


def solution(mesh):
    fine = Mesh(mesh.devices.reshape(mesh.devices.shape[0], NY, NZ, NX, NC), ("dp", "y", "z", "x", "core"))
    rows, heads = ("dp", "y", "z"), ("x", "core")
    in_specs = (
        P(rows, heads),
        P(rows, heads),
        P(rows, heads),
        P(heads, None),
        P("dp"),
        P("dp"),
        P("dp", None),
        P("dp"),
    )
    return jax.shard_map(per_device, mesh=fine, in_specs=in_specs, out_specs=P(rows, heads), check_vma=False)
```
